32 devices in a mesh: dp: 8 (over y, x, core), tensor: 4 (over z).
Axes of the slice: x: 2, y: 2, z: 4, core: 2. Of those that a mesh axis runs over, the one named last changes fastest.
Arguments:
- layer_input: bfloat16 [4096, 8192], P('dp', 'tensor'), may hold values from -180 to 180
- gain: bfloat16 [8192], P('tensor'), may hold values from 0.25 to 1.75
- w_kv: bfloat16 [2048, 8192], P(None, 'tensor'), may hold values from -0.125 to 0.125
- d_kv: bfloat16 [4096, 2048], P('dp', 'tensor'), may hold values from -12 to 12
- destination: int32 [4096], P('dp'), may hold values from -1 to 7, as said below
Outputs:
- grad_x: bfloat16 [4096, 8192], P('dp', 'tensor')
- grad_weight: float32 [2048, 8192], P('dp', 'tensor')
The draws below stay inside these ranges and needn't reach their ends.
Inputs may be any that keep to these rules, and one draw needn't show every extreme that they name: The rows of one device with destination >= 0 are its first rows, 128 of them or more, and some device has no padding. At most 64 rows of one device name the same destination, and some destination is named by exactly 64 rows of every device.
All inputs are finite; a program needn't handle non-finite values.
Results may differ from the reference program's by a relative error of at most 0.0031.
Values may be sent and summed in bfloat16 or wider, within the bound.
A program may use at most 64 MiB of HBM per device.

```python
import jax
import jax.numpy as jnp
from jax import lax

D = 8192
TOK_DEV = 512
KVW = 1024
ROWS_PEER = 64
TOKENS = 4096
N_DP = 8


def draw_layer_input(key, part):
    key_a, key_b, key_c = jax.random.split(jax.random.fold_in(key, 11), 3)
    column = jnp.arange(D, dtype=jnp.float32) / D
    column_scale = jnp.exp(jnp.log(3.0) * column) * jnp.exp(jnp.log(10.0) * jax.random.uniform(key_a, (D,), jnp.float32))
    row_scale = jnp.exp(jnp.log(10.0) * jax.random.uniform(key_b, (TOKENS, 1), jnp.float32))
    noise = jnp.clip(jax.random.normal(key_c, (TOKENS, D), jnp.float32), -6.0, 6.0)
    return (noise * column_scale * row_scale / 10.0).astype(jnp.bfloat16)


def draw_destination(key, part):
    base_key = jax.random.fold_in(key, 23)
    key_len, key_full, key_star, key_rows = jax.random.split(base_key, 4)
    lengths = jax.random.randint(key_len, (N_DP,), TOK_DEV // 4, TOK_DEV + 1)
    full_dev = jax.random.randint(key_full, (), 0, N_DP)
    lengths = jnp.where(jnp.arange(N_DP) == full_dev, TOK_DEV, lengths)
    star_dev = jax.random.randint(key_star, (), 0, N_DP)
    slot_dest = jnp.arange(TOK_DEV, dtype=jnp.int32) // ROWS_PEER
    row_ids = jnp.arange(TOK_DEV, dtype=jnp.int32)

    def one_device(device_key, length):
        key_order, key_shuffle = jax.random.split(device_key)
        order_perm = jax.random.permutation(key_order, TOK_DEV).astype(jnp.int32)
        priority = jnp.where(slot_dest == star_dev, 0, TOK_DEV) + order_perm
        chosen = jnp.argsort(priority)
        shuffle = jax.random.permutation(key_shuffle, TOK_DEV).astype(jnp.int32)
        is_live = row_ids < length
        below = (shuffle[None, :] < shuffle[:, None]) & is_live[None, :]
        live_rank = jnp.sum(below.astype(jnp.int32), axis=1)
        picked = chosen[jnp.minimum(live_rank, TOK_DEV - 1)]
        return jnp.where(is_live, slot_dest[picked], -1)
    dev_keys = jax.random.split(key_rows, N_DP)
    return jax.vmap(one_device)(dev_keys, lengths).reshape(TOKENS).astype(jnp.int32)


def spiked(entries, key, source, target, blocks, factor):
    def block_of(dim):
        return (jnp.arange(entries.shape[dim]) // (entries.shape[dim] // blocks)).reshape((-1,) + (1,) * (entries.ndim - 1 - dim))

    near = jax.random.permutation(key, blocks)[block_of(target)]
    second = (block_of(target) + blocks // 2) % blocks
    return jnp.where((block_of(source) == near) | (block_of(source) == second), factor * entries, entries)


def levels(rng, extent, pieces, least, largest):
    factor_of, own = 1.0, jax.random.fold_in(rng, 6)
    for axis_at, blocks in pieces:
        heights = jnp.exp(jax.random.uniform(jax.random.fold_in(own, axis_at), (blocks,), jnp.float32, least / len(pieces), largest / len(pieces)))
        factor_of = factor_of * jnp.repeat(heights, extent[axis_at] // blocks).reshape([-1 if axis == axis_at else 1 for axis in range(len(extent))])
    return factor_of


def gaussian(stream_key, extent, width, most, pieces=(), kind=jnp.bfloat16):
    array = jax.random.normal(stream_key, extent, jnp.float32) * width
    if len(pieces) > 0:
        array = levels(stream_key, extent, pieces, -0.22, 0.18) * array
    return jnp.clip(array, min=-most, max=most).astype(kind)


def gaussian_with(stream_key, dims, spread, most, shards, heavy, kind=jnp.bfloat16):
    array = spread * jax.random.normal(stream_key, dims, jnp.float32)
    if shards:
        array = array * levels(stream_key, dims, shards, -0.22, 0.18)
    return jnp.clip(spiked(array, jax.random.fold_in(stream_key, 3), *heavy), -most, most).astype(kind)


def setup_inputs(seed: int = 0) -> dict:
    streams_of = jax.random.split(jax.random.key(seed), 6)
    layer_input = draw_layer_input(jax.random.fold_in(streams_of[5], 71), 0)
    gain = jnp.clip(1.0 + 0.15 * jax.random.normal(streams_of[1], (D,), jnp.float32), 0.25, 1.75).astype(jnp.bfloat16)
    w_kv = gaussian(streams_of[2], (2 * KVW, D), (2 * KVW) ** -0.5, 0.125, ((1, 4),))
    d_kv = gaussian_with(streams_of[3], (TOKENS, 2 * KVW), 2.0, 12.0, ((0, 8), (1, 4)), (0, 1, 8, 2.0))
    destination = draw_destination(jax.random.fold_in(streams_of[5], 71), 0)
    return {"layer_input": layer_input, "gain": gain, "w_kv": w_kv, "d_kv": d_kv, "destination": destination}


EPS = 1e-06

def reference(layer_input, gain, w_kv, d_kv, destination):
    peer_ids = jnp.arange(N_DP, dtype=jnp.int32)
    gain_wide = gain.astype(jnp.float32)

    def owner_block(weight_acc, owner_idx):
        block_rows = lax.dynamic_slice_in_dim(layer_input, owner_idx * TOK_DEV, TOK_DEV, 0)
        target = lax.dynamic_slice_in_dim(destination, owner_idx * TOK_DEV, TOK_DEV, 0)
        onehot = (target[:, None] == peer_ids[None, :]).astype(jnp.int32)
        before = jnp.cumsum(onehot, axis=0) - onehot
        slot_rank = lax.optimization_barrier(jnp.sum(before * onehot, axis=1))
        is_live = target >= 0
        slot_index = jnp.where(is_live, target * TOK_DEV + owner_idx * ROWS_PEER + slot_rank, 0).astype(jnp.int32)
        cotangent = jnp.where(is_live[:, None], d_kv[slot_index], jnp.zeros((), d_kv.dtype))
        values = block_rows.astype(jnp.float32)
        inverse = lax.rsqrt(lax.optimization_barrier(jnp.mean(values * values, axis=1)) + EPS)
        normed = (values * inverse[:, None] * gain_wide).astype(jnp.bfloat16)
        dnormed = jnp.dot(cotangent, w_kv, preferred_element_type=jnp.float32)
        mean_dot = lax.optimization_barrier(jnp.mean(values * gain_wide * dnormed, axis=1))
        grad_rows = (inverse[:, None] * gain_wide * dnormed - values * (inverse ** 3 * mean_dot)[:, None]).astype(jnp.bfloat16)
        term = lax.dot_general(cotangent, normed, (((0,), (0,)), ((), ())), preferred_element_type=jnp.float32)
        return (weight_acc + term, grad_rows)
    weight, grads = lax.scan(owner_block, jnp.zeros((2 * KVW, D), jnp.float32), jnp.arange(N_DP, dtype=jnp.int32))
    return (grads.reshape(TOKENS, D), weight)
```

```python
import functools

import jax
import jax.numpy as jnp
from jax import lax
from jax.experimental import pallas as pl
from jax.experimental.pallas import tpu as pltpu
from jax.sharding import PartitionSpec as P

D = 8192
EPS = 1e-06
BF = jnp.bfloat16
F32 = jnp.float32


def chip_grid(dp_count):
    chips = dp_count // 2
    width = 1 << ((chips.bit_length() - 1) // 2)
    return chips // width, width


def weight_kernel(height, width, cot_ref, normed_ref, out_ref, rcot, rnormed,
                  sxa, rxa, sya, rya, sxb, rxb, syb, ryb,
                  pair_send, pair_recv, xa_s, xa_r, ya_s, ya_r, xb_s, xb_r, yb_s, yb_r):
    me = lax.axis_index("dp")
    core = lax.rem(me, 2)
    chip = me // 2
    row, col = chip // width, lax.rem(chip, width)
    sibling = me + 1 - 2 * core
    block, features = out_ref.shape
    half = features // 2
    tile = min(256, half)

    def device(r, c):
        return {"dp": (r * width + c) * 2 + core}

    def shift_row(d):
        return lax.rem(row + d, height)

    def shift_col(d):
        return lax.rem(col + d, width)

    barrier = pltpu.get_barrier_semaphore()
    pl.semaphore_signal(barrier, inc=1, device_id={"dp": sibling}, device_id_type=pl.DeviceIdType.MESH)
    for d in range(1, width):
        pl.semaphore_signal(barrier, inc=1, device_id=device(row, shift_col(d)), device_id_type=pl.DeviceIdType.MESH)
    for d in range(1, height):
        pl.semaphore_signal(barrier, inc=1, device_id=device(shift_row(d), col), device_id_type=pl.DeviceIdType.MESH)
    pl.semaphore_wait(barrier, 1 + width - 1 + height - 1)

    def send(src, dst, s, r, dev):
        copy = pltpu.make_async_remote_copy(src_ref=src, dst_ref=dst, send_sem=s, recv_sem=r, device_id=dev,
                                            device_id_type=pl.DeviceIdType.MESH)
        copy.start()
        return copy

    pair = [
        send(cot_ref.at[1 - core], rcot, pair_send.at[0], pair_recv.at[0], {"dp": sibling}),
        send(normed_ref, rnormed, pair_send.at[1], pair_recv.at[1], {"dp": sibling}),
    ]
    for copy in pair:
        copy.wait()

    def product(r, c, first, store):
        index = r * width + c

        def step(i, carry):
            at = pl.ds(pl.multiple_of(i * tile, tile), tile)
            wide = pl.ds(pl.multiple_of(first + i * tile, tile), tile)
            value = jnp.dot(cot_ref[core, index], normed_ref[:, wide], preferred_element_type=F32)
            value += jnp.dot(rcot[index], rnormed[:, wide], preferred_element_type=F32)
            store(at, wide, value)
            return carry

        lax.fori_loop(0, half // tile, step, 0)

    def into(ref):
        def store(at, wide, value):
            ref[:, at] = value.astype(BF)
        return store

    first_x, first_y = {}, {}
    for dr in list(range(1, height)) + [0]:
        for dc in range(1, width):
            product(shift_row(dr), shift_col(dc), 0, into(sxa.at[dc - 1, dr]))
            first_x[dc, dr] = send(sxa.at[dc - 1, dr], rxa.at[dc - 1, dr], xa_s.at[dc - 1, dr], xa_r.at[dc - 1, dr],
                                   device(row, shift_col(dc)))
        if dr > 0:
            for dc in list(range(1, width)):
                product(shift_row(dr), shift_col(dc), half, into(sya.at[dr - 1, dc]))
                first_y[dr, dc] = send(sya.at[dr - 1, dc], rya.at[dr - 1, dc], ya_s.at[dr - 1, dc],
                                       ya_r.at[dr - 1, dc], device(shift_row(dr), col))
    for dr in range(1, height):
        product(shift_row(dr), col, half, into(sya.at[dr - 1, 0]))
        first_y[dr, 0] = send(sya.at[dr - 1, 0], rya.at[dr - 1, 0], ya_s.at[dr - 1, 0], ya_r.at[dr - 1, 0],
                              device(shift_row(dr), col))

    def keep(at, wide, value):
        out_ref[:, wide] = value

    product(row, col, 0, keep)
    product(row, col, half, keep)

    second = []
    for dr in range(1, height):
        for dc in range(1, width):
            first_x[dc, dr].wait_recv()

        def store(at, wide, value, dr=dr):
            for dc in range(1, width):
                value += rxa[dc - 1, dr, :, at].astype(F32)
            syb[dr - 1, :, at] = value.astype(BF)

        product(shift_row(dr), col, 0, store)
        second.append(send(syb.at[dr - 1], ryb.at[dr - 1], yb_s.at[dr - 1], yb_r.at[dr - 1],
                           device(shift_row(dr), col)))
    for dc in range(1, width):
        for dr in range(1, height):
            first_y[dr, dc].wait_recv()

        def store(at, wide, value, dc=dc):
            for dr in range(1, height):
                value += rya[dr - 1, dc, :, at].astype(F32)
            sxb[dc - 1, :, at] = value.astype(BF)

        product(row, shift_col(dc), half, store)
        second.append(send(sxb.at[dc - 1], rxb.at[dc - 1], xb_s.at[dc - 1], xb_r.at[dc - 1],
                           device(row, shift_col(dc))))

    for dc in range(1, width):
        first_x[dc, 0].wait_recv()
    for dr in range(1, height):
        first_y[dr, 0].wait_recv()
    for copy in second:
        copy.wait_recv()

    def finish(i, carry):
        at = pl.ds(pl.multiple_of(i * tile, tile), tile)
        wide = pl.ds(pl.multiple_of(half + i * tile, tile), tile)
        left, right = out_ref[:, at], out_ref[:, wide]
        for dc in range(1, width):
            left += rxa[dc - 1, 0, :, at].astype(F32)
            right += rxb[dc - 1, :, at].astype(F32)
        for dr in range(1, height):
            left += ryb[dr - 1, :, at].astype(F32)
            right += rya[dr - 1, 0, :, at].astype(F32)
        out_ref[:, at] = left
        out_ref[:, wide] = right
        return carry

    lax.fori_loop(0, half // tile, finish, 0)
    for copy in list(first_x.values()) + list(first_y.values()) + second:
        copy.wait_send()


def weight_gradient(dp_count, cot_cores, normed):
    height, width = chip_grid(dp_count)
    cores, chips, block, rows = cot_cores.shape
    features = normed.shape[1]
    half = features // 2
    dma = pltpu.SemaphoreType.DMA
    return pl.pallas_call(
        functools.partial(weight_kernel, height, width),
        out_shape=jax.ShapeDtypeStruct((block, features), F32),
        in_specs=[pl.BlockSpec(memory_space=pltpu.VMEM)] * 2,
        out_specs=pl.BlockSpec(memory_space=pltpu.VMEM),
        scratch_shapes=[
            pltpu.VMEM((chips, block, rows), BF),
            pltpu.VMEM((rows, features), BF),
            pltpu.VMEM((width - 1, height, block, half), BF),
            pltpu.VMEM((width - 1, height, block, half), BF),
            pltpu.VMEM((height - 1, width, block, half), BF),
            pltpu.VMEM((height - 1, width, block, half), BF),
            pltpu.VMEM((width - 1, block, half), BF),
            pltpu.VMEM((width - 1, block, half), BF),
            pltpu.VMEM((height - 1, block, half), BF),
            pltpu.VMEM((height - 1, block, half), BF),
            dma((2,)), dma((2,)),
            dma((width - 1, height)), dma((width - 1, height)),
            dma((height - 1, width)), dma((height - 1, width)),
            dma((width - 1,)), dma((width - 1,)),
            dma((height - 1,)), dma((height - 1,)),
        ],
        compiler_params=pltpu.CompilerParams(collective_id=0, has_side_effects=True,
                                             vmem_limit_bytes=40 * 1024 * 1024),
    )(cot_cores, normed)


def shards(layer_input, gain, w_kv, d_kv, destination):
    dp_count = lax.axis_size("dp")
    row_count = destination.shape[0]
    peer_rows = row_count // dp_count
    columns = d_kv.shape[1]
    slots = lax.all_to_all(d_kv.reshape(dp_count, peer_rows, columns), "dp", split_axis=0, concat_axis=0,
                           tiled=True).reshape(row_count, columns)
    slots = lax.all_gather(slots, "tensor", axis=1, tiled=True)
    values = layer_input.astype(F32)
    gain_wide = gain.astype(F32)
    squares = lax.psum(jnp.sum(values * values, axis=1), "tensor")
    peer_ids = jnp.arange(dp_count, dtype=jnp.int32)
    onehot = (destination[:, None] == peer_ids[None, :]).astype(jnp.int32)
    before = jnp.cumsum(onehot, axis=0) - onehot
    position = jnp.where(destination >= 0, destination * peer_rows + jnp.sum(before * onehot, axis=1), -1)
    place = (position[:, None] == jnp.arange(row_count, dtype=jnp.int32)[None, :]).astype(BF)
    cot = jnp.dot(place, slots, preferred_element_type=F32).astype(BF)
    inverse = lax.rsqrt(squares / D + EPS)
    normed = (values * inverse[:, None] * gain_wide).astype(BF)
    dnormed = jnp.dot(cot, w_kv, preferred_element_type=F32)
    products = lax.psum(jnp.sum(values * gain_wide * dnormed, axis=1), "tensor")
    grad_x = (inverse[:, None] * gain_wide * dnormed
              - values * (inverse**3 * (products / D))[:, None]).astype(BF)
    total = cot.shape[1]
    block = total // dp_count
    cot_cores = cot.T.reshape(dp_count // 2, 2, block, row_count).transpose(1, 0, 2, 3)
    return (grad_x, weight_gradient(dp_count, cot_cores, normed))


def solution(mesh):
    return jax.shard_map(
        shards,
        mesh=mesh,
        in_specs=(P("dp", "tensor"), P("tensor"), P(None, "tensor"), P("dp", "tensor"), P("dp")),
        out_specs=(P("dp", "tensor"), P("dp", "tensor")),
        check_vma=False,
    )
```

```python
import functools

import jax
import jax.numpy as jnp
from jax import lax
from jax.experimental import pallas as pl
from jax.experimental.pallas import tpu as pltpu
from jax.sharding import PartitionSpec as P

D = 8192
EPS = 1e-06
BF = jnp.bfloat16
F32 = jnp.float32


def chip_grid(dp_count):
    chips = dp_count // 2
    width = 1 << ((chips.bit_length() - 1) // 2)
    return chips // width, width


MESH = pl.DeviceIdType.MESH
GROUPS = 4


def kernel(shape, x_hbm, gain_ref, w_hbm, dkv_hbm, dest_ref, gx_hbm, gw_hbm,
           x, w, slots, place, place_t, cot_buf, cot_t, rcot, normed, rnormed, dnormed, gx, total,
           lanes, inv_col, fac_col, sstat, rstat,
           sxa, rxa, sya, rya, sxb, rxb, syb, ryb,
           load_sem, store_sem, own_sem, a2a_s, a2a_r, right_s, right_r, left_s, left_r, stat_s, stat_r,
           pair_s, pair_r, nrm_s, nrm_r, xa_s, xa_r, ya_s, ya_r, xb_s, xb_r, yb_s, yb_r):
    dp_count, depth, height, width = shape
    me = lax.axis_index("dp")
    z = lax.axis_index("tensor")
    core = lax.rem(me, 2)
    chip = me // 2
    row, col = chip // width, lax.rem(chip, width)
    sibling = me + 1 - 2 * core
    rows, features = x.shape
    columns = slots.shape[3]
    peer_rows = slots.shape[2]
    block = total.shape[0]
    half = features // 2
    tile = min(256, half)
    chips_each = (dp_count // 2) // depth
    piece = dp_count // GROUPS

    def remote(src, dst, s, r, dev):
        return pltpu.make_async_remote_copy(src_ref=src, dst_ref=dst, send_sem=s, recv_sem=r, device_id=dev,
                                            device_id_type=MESH)

    def device(r, c):
        return {"dp": (r * width + c) * 2 + core}

    def shift_row(d):
        return lax.rem(row + d, height)

    def shift_col(d):
        return lax.rem(col + d, width)

    load_x = pltpu.make_async_copy(x_hbm, x, load_sem.at[0])
    load_w = pltpu.make_async_copy(w_hbm, w, load_sem.at[1])
    own = pltpu.make_async_copy(dkv_hbm.at[me], slots.at[z, 0], own_sem)
    own.start()
    load_x.start()
    load_w.start()

    barrier = pltpu.get_barrier_semaphore()
    for d in range(1, dp_count):
        pl.semaphore_signal(barrier, inc=1, device_id={"dp": lax.rem(me + d, dp_count)}, device_id_type=MESH)
    for d in range(1, depth):
        pl.semaphore_signal(barrier, inc=1, device_id={"tensor": lax.rem(z + d, depth)}, device_id_type=MESH)
    pl.semaphore_wait(barrier, dp_count - 1 + depth - 1)

    def cot_copy(d):
        peer = lax.rem(me + d, dp_count)
        return remote(dkv_hbm.at[peer], slots.at[z, d], a2a_s.at[d - 1], a2a_r.at[d - 1], {"dp": peer})

    for d in range(1, dp_count):
        cot_copy(d).start()

    def right_copy(step, g):
        ref = slots.at[z - step, pl.ds(g * piece, piece)]
        return remote(ref, ref, right_s.at[step, g], right_r.at[step, g], {"tensor": z + 1})

    def left_copy(step, g):
        ref = slots.at[z + step, pl.ds(g * piece, piece)]
        return remote(ref, ref, left_s.at[step, g], left_r.at[step, g], {"tensor": z - 1})

    def wait_right(step, g):
        ref = slots.at[z - step, pl.ds(g * piece, piece)]
        remote(ref, ref, right_s.at[step, g], right_r.at[step - 1, g], {"tensor": z - 1}).wait_recv()

    def wait_left(step, g):
        ref = slots.at[z + step, pl.ds(g * piece, piece)]
        remote(ref, ref, left_s.at[step, g], left_r.at[step - 1, g], {"tensor": z + 1}).wait_recv()

    for g in range(GROUPS):
        for d in range(g * piece, (g + 1) * piece):
            if d == 0:
                own.wait()
            else:
                cot_copy(d).wait_recv()

        @pl.when(z < depth - 1)
        def _(g=g):
            right_copy(0, g).start()

        @pl.when(z > 0)
        def _(g=g):
            left_copy(0, g).start()

    chunk = 64

    def over_tiles(body, wide):
        def outer(i, carry):
            at = pl.ds(pl.multiple_of(i * chunk, chunk), chunk)

            def inner(j, inner_carry):
                body(at, pl.ds(pl.multiple_of(j * wide, wide), wide))
                return inner_carry

            return lax.fori_loop(0, features // wide, inner, carry)

        lax.fori_loop(0, rows // chunk, outer, 0)

    def row_sums(body, which):
        def outer(i, carry):
            at = pl.ds(pl.multiple_of(i * chunk, chunk), chunk)

            def inner(j, acc):
                return acc + body(at, pl.ds(pl.multiple_of(j * 128, 128), 128))

            lanes[at, :] = lax.fori_loop(0, features // 128, inner, jnp.zeros((chunk, 128), F32), unroll=4)
            return carry

        lax.fori_loop(0, rows // chunk, outer, 0)
        sums = jnp.sum(lanes[...].T, axis=0, keepdims=True)
        sstat[which] = jnp.broadcast_to(sums, (8, rows))
        for d in range(1, depth):
            stat_copy(which, d).start()

    def stat_copy(which, d):
        return remote(sstat.at[which], rstat.at[which, d - 1], stat_s.at[which, d - 1], stat_r.at[which, d - 1],
                      {"tensor": lax.rem(z + d, depth)})

    def row_total(which):
        value = sstat[which]
        for d in range(1, depth):
            stat_copy(which, d).wait_recv()
            value += rstat[which, d - 1]
        return value[0:1, :]

    def as_column(value):
        return jnp.broadcast_to(value, (128, rows)).T

    load_x.wait()

    def square(at, wide):
        values = x[at, wide].astype(F32)
        return values * values

    row_sums(square, 0)

    dest = dest_ref[...]
    dest_col = as_column(dest.astype(F32))[:, 0:1]
    first = lax.broadcasted_iota(jnp.int32, (rows, rows), 0)
    second_axis = lax.broadcasted_iota(jnp.int32, (rows, rows), 1)
    same = (dest_col == dest.astype(F32)) & (first < second_axis)
    rank = jnp.sum(jnp.where(same, 1.0, 0.0), axis=0, keepdims=True)
    offset = me - dest
    offset = jnp.where(offset < 0, offset + dp_count, offset)
    position = jnp.where(dest >= 0, offset.astype(F32) * peer_rows + rank, -1.0)
    place_t[...] = jnp.where(position.astype(jnp.int32) == first, 1.0, 0.0).astype(BF)
    position_col = as_column(position)[:, 0:1].astype(jnp.int32)
    place[...] = jnp.where(position_col == second_axis, 1.0, 0.0).astype(BF)

    def pair_copy(index):
        return remote(cot_t.at[index, 1 - core], rcot.at[index], pair_s.at[index], pair_r.at[index], {"dp": sibling})

    def consume(b, fresh):
        block_slots = slots[b].reshape(rows, columns)
        cot_rows = lax.dot_general(block_slots, place_t[...], (((0,), (0,)), ((), ())),
                                   preferred_element_type=F32).astype(BF)
        for q in range(chips_each):
            for c in range(2):
                start = (q * 2 + c) * block
                cot_t[b * chips_each + q, c] = cot_rows[start:start + block]
            pair_copy(b * chips_each + q).start()
        cot_buf[...] = jnp.dot(place[...], block_slots, preferred_element_type=F32).astype(BF)

        def step(i, carry):
            at = pl.ds(pl.multiple_of(i * tile, tile), tile)
            value = jnp.dot(cot_buf[...], w[b, :, at], preferred_element_type=F32)
            if fresh:
                dnormed[:, at] = value
            else:
                dnormed[:, at] += value
            return carry

        lax.fori_loop(0, features // tile, step, 0)

    def product(index, start, store):
        def step(i, carry):
            at = pl.ds(pl.multiple_of(i * tile, tile), tile)
            wide = pl.ds(pl.multiple_of(start + i * tile, tile), tile)
            value = jnp.dot(cot_t[index, core], normed[:, wide], preferred_element_type=F32)
            value += jnp.dot(rcot[index], rnormed[:, wide], preferred_element_type=F32)
            store(at, wide, value)
            return carry

        lax.fori_loop(0, half // tile, step, 0)

    def xa_copy(dc, dr):
        return remote(sxa.at[dc - 1, dr], rxa.at[dc - 1, dr], xa_s.at[dc - 1, dr], xa_r.at[dc - 1, dr],
                      device(row, shift_col(dc)))

    def ya_copy(dr, dc):
        return remote(sya.at[dr - 1, dc], rya.at[dr - 1, dc], ya_s.at[dr - 1, dc], ya_r.at[dr - 1, dc],
                      device(shift_row(dr), col))

    def xb_copy(dc):
        return remote(sxb.at[dc - 1], rxb.at[dc - 1], xb_s.at[dc - 1], xb_r.at[dc - 1], device(row, shift_col(dc)))

    def yb_copy(dr):
        return remote(syb.at[dr - 1], ryb.at[dr - 1], yb_s.at[dr - 1], yb_r.at[dr - 1], device(shift_row(dr), col))

    def contribute(b):
        for q in range(chips_each):
            index = b * chips_each + q
            dr = lax.rem(index // width - row + height, height)
            dc = lax.rem(lax.rem(index, width) - col + width, width)
            pair_copy(index).wait_recv()

            @pl.when(dc > 0)
            def _():
                def store(at, wide, value):
                    sxa[dc - 1, dr, :, at] = value.astype(BF)

                product(index, 0, store)
                xa_copy(dc, dr).start()

            @pl.when(dr > 0)
            def _():
                def store(at, wide, value):
                    sya[dr - 1, dc, :, at] = value.astype(BF)

                product(index, half, store)
                ya_copy(dr, dc).start()

    load_w.wait()
    consume(z, True)

    inverse = lax.rsqrt(row_total(0) / D + EPS)
    inv_col[...] = as_column(inverse)

    def normalize(at, wide):
        values = x[at, wide].astype(F32)
        normed[at, wide] = (values * inv_col[at, 0:1] * gain_ref[:, wide].astype(F32)).astype(BF)

    wide_tile = min(512, features)
    over_tiles(normalize, wide_tile)
    share = remote(normed, rnormed, nrm_s, nrm_r, {"dp": sibling})
    share.start()

    def chain(step, carry):
        for g in range(GROUPS):
            @pl.when(z - step >= 0)
            def _(g=g):
                wait_right(step, g)

                @pl.when(z < depth - 1)
                def _():
                    right_copy(step, g).start()

            @pl.when(z + step <= depth - 1)
            def _(g=g):
                wait_left(step, g)

                @pl.when(z > 0)
                def _():
                    left_copy(step, g).start()

        @pl.when(z - step >= 0)
        def _():
            consume(z - step, False)

        @pl.when(z + step <= depth - 1)
        def _():
            consume(z + step, False)

        @pl.when(step == 1)
        def _():
            share.wait_recv()

        @pl.when(z - step + 1 >= 0)
        def _():
            contribute(z - step + 1)

        @pl.when((step > 1) & (z + step - 1 <= depth - 1))
        def _():
            contribute(z + step - 1)

        return carry

    lax.fori_loop(1, depth, chain, 0)

    @pl.when(z == depth - 1)
    def _():
        contribute(0)

    @pl.when(z == 0)
    def _():
        contribute(depth - 1)

    def dotted(at, wide):
        return x[at, wide].astype(F32) * gain_ref[:, wide].astype(F32) * dnormed[at, wide]

    row_sums(dotted, 1)

    def keep(at, wide, value):
        total[:, wide] = value

    product(chip, 0, keep)
    product(chip, half, keep)

    for dr in range(1, height):
        for dc in range(1, width):
            xa_copy(dc, dr).wait_recv()

        def store(at, wide, value, dr=dr):
            for dc in range(1, width):
                value += rxa[dc - 1, dr, :, at].astype(F32)
            syb[dr - 1, :, at] = value.astype(BF)

        product(shift_row(dr) * width + col, 0, store)
        yb_copy(dr).start()
    for dc in range(1, width):
        for dr in range(1, height):
            ya_copy(dr, dc).wait_recv()

        def store(at, wide, value, dc=dc):
            for dr in range(1, height):
                value += rya[dr - 1, dc, :, at].astype(F32)
            sxb[dc - 1, :, at] = value.astype(BF)

        product(row * width + shift_col(dc), half, store)
        xb_copy(dc).start()

    inverse_row = lax.rsqrt(row_total_done(sstat, rstat, depth) / D + EPS)
    fac_col[...] = as_column(inverse_row**3 * (row_total(1) / D))

    def gradient(at, wide):
        values = x[at, wide].astype(F32)
        gx[at, wide] = (inv_col[at, 0:1] * gain_ref[:, wide].astype(F32) * dnormed[at, wide]
                        - values * fac_col[at, 0:1]).astype(BF)

    over_tiles(gradient, wide_tile)
    store_gx = pltpu.make_async_copy(gx, gx_hbm, store_sem.at[0])
    store_gx.start()

    for dc in range(1, width):
        xa_copy(dc, 0).wait_recv()
        xb_copy(dc).wait_recv()
    for dr in range(1, height):
        ya_copy(dr, 0).wait_recv()
        yb_copy(dr).wait_recv()

    def finish(i, carry):
        at = pl.ds(pl.multiple_of(i * tile, tile), tile)
        wide = pl.ds(pl.multiple_of(half + i * tile, tile), tile)
        left, right = total[:, at], total[:, wide]
        for dc in range(1, width):
            left += rxa[dc - 1, 0, :, at].astype(F32)
            right += rxb[dc - 1, :, at].astype(F32)
        for dr in range(1, height):
            left += ryb[dr - 1, :, at].astype(F32)
            right += rya[dr - 1, 0, :, at].astype(F32)
        total[:, at] = left
        total[:, wide] = right
        return carry

    lax.fori_loop(0, half // tile, finish, 0)
    store_gw = pltpu.make_async_copy(total, gw_hbm, store_sem.at[1])
    store_gw.start()

    for d in range(1, dp_count):
        cot_copy(d).wait_send()
    for which in range(2):
        for d in range(1, depth):
            stat_copy(which, d).wait_send()

    def drain(step, carry):
        for g in range(GROUPS):
            @pl.when((z - step >= 0) & (z < depth - 1))
            def _(g=g):
                right_copy(step, g).wait_send()

            @pl.when((z + step <= depth - 1) & (z > 0))
            def _(g=g):
                left_copy(step, g).wait_send()

        return carry

    lax.fori_loop(0, depth, drain, 0)
    share.wait_send()
    for index in range(dp_count // 2):
        pair_copy(index).wait_send()
    for dc in range(1, width):
        for dr in range(height):
            xa_copy(dc, dr).wait_send()
        xb_copy(dc).wait_send()
    for dr in range(1, height):
        for dc in range(width):
            ya_copy(dr, dc).wait_send()
        yb_copy(dr).wait_send()
    store_gx.wait()
    store_gw.wait()


def row_total_done(sstat, rstat, depth):
    value = sstat[0]
    for d in range(1, depth):
        value += rstat[0, d - 1]
    return value[0:1, :]


def shards(layer_input, gain, w_kv, d_kv, destination):
    dp_count, depth = lax.axis_size("dp"), lax.axis_size("tensor")
    height, width = chip_grid(dp_count)
    rows, features = layer_input.shape
    columns = d_kv.shape[1]
    chips = dp_count // 2
    block = w_kv.shape[0] // dp_count
    half = features // 2
    dma, vmem = pltpu.SemaphoreType.DMA, pltpu.VMEM
    anywhere = pl.BlockSpec(memory_space=pl.ANY)
    inside = pl.BlockSpec(memory_space=pltpu.VMEM)
    return pl.pallas_call(
        functools.partial(kernel, (dp_count, depth, height, width)),
        out_shape=(jax.ShapeDtypeStruct((rows, features), BF), jax.ShapeDtypeStruct((block, features), F32)),
        in_specs=[anywhere, inside, anywhere, anywhere, inside],
        out_specs=(anywhere, anywhere),
        scratch_shapes=[
            vmem((rows, features), BF),
            vmem((depth, columns, features), BF),
            vmem((depth, dp_count, rows // dp_count, columns), BF),
            vmem((rows, rows), BF),
            vmem((rows, rows), BF),
            vmem((rows, columns), BF),
            vmem((chips, 2, block, rows), BF),
            vmem((chips, block, rows), BF),
            vmem((rows, features), BF),
            vmem((rows, features), BF),
            vmem((rows, features), F32),
            vmem((rows, features), BF),
            vmem((block, features), F32),
            vmem((rows, 128), F32),
            vmem((rows, 128), F32),
            vmem((rows, 128), F32),
            vmem((2, 8, rows), F32),
            vmem((2, depth - 1, 8, rows), F32),
            vmem((width - 1, height, block, half), BF),
            vmem((width - 1, height, block, half), BF),
            vmem((height - 1, width, block, half), BF),
            vmem((height - 1, width, block, half), BF),
            vmem((width - 1, block, half), BF),
            vmem((width - 1, block, half), BF),
            vmem((height - 1, block, half), BF),
            vmem((height - 1, block, half), BF),
            dma((2,)), dma((2,)), dma,
            dma((dp_count - 1,)), dma((dp_count - 1,)),
            dma((depth, GROUPS)), dma((depth, GROUPS)), dma((depth, GROUPS)), dma((depth, GROUPS)),
            dma((2, depth - 1)), dma((2, depth - 1)),
            dma((chips,)), dma((chips,)), dma, dma,
            dma((width - 1, height)), dma((width - 1, height)),
            dma((height - 1, width)), dma((height - 1, width)),
            dma((width - 1,)), dma((width - 1,)),
            dma((height - 1,)), dma((height - 1,)),
        ],
        compiler_params=pltpu.CompilerParams(collective_id=0, has_side_effects=True,
                                             vmem_limit_bytes=56 * 1024 * 1024),
    )(layer_input, gain.reshape(1, features), w_kv.reshape(depth, columns, features),
      d_kv.reshape(dp_count, rows // dp_count, columns), destination.reshape(1, rows))


def solution(mesh):
    return jax.shard_map(
        shards,
        mesh=mesh,
        in_specs=(P("dp", "tensor"), P("tensor"), P(None, "tensor"), P("dp", "tensor"), P("dp")),
        out_specs=(P("dp", "tensor"), P("dp", "tensor")),
        check_vma=False,
    )
```

```python
import functools

import jax
import jax.numpy as jnp
from jax import lax
from jax.experimental import pallas as pl
from jax.experimental.pallas import tpu as pltpu
from jax.sharding import PartitionSpec as P

D = 8192
EPS = 1e-06
BF = jnp.bfloat16
F32 = jnp.float32


def chip_grid(dp_count):
    chips = dp_count // 2
    width = 1 << ((chips.bit_length() - 1) // 2)
    return chips // width, width


MESH = pl.DeviceIdType.MESH
LANES = 128


def kernel(shape, x_hbm, gain_ref, w_hbm, dkv_hbm, dest_ref, gx_hbm, gw_hbm,
           x, w, slots, place, place_t, cot_buf, cot_t, rcot, normed, rnormed, dnormed, gx, total,
           lanes, inv_col, fac_col, sstat, rstat,
           sxa, rxa, sya, rya, sxb, rxb, syb, ryb,
           load_sem, load_w_sem, store_sem, own_sem, a2a_s, a2a_r, right_s, right_r, left_s, left_r, stat_s, stat_r,
           pair_s, pair_r, nrm_s, nrm_r, xa_s, xa_r, ya_s, ya_r, xb_s, xb_r, yb_s, yb_r):
    dp_count, depth, height, width = shape
    me = lax.axis_index("dp")
    z = lax.axis_index("tensor")
    core = lax.rem(me, 2)
    chip = me // 2
    row, col = chip // width, lax.rem(chip, width)
    sibling = me + 1 - 2 * core
    rows, features = x.shape
    parts, lists, peer_rows, span = slots.shape[1], slots.shape[2], slots.shape[4], slots.shape[5]
    order = [(h, k) for h in range(parts) for k in range(lists)]
    block = total.shape[0]
    half = features // 2
    tile = min(256, half)
    chips_each = (dp_count // 2) // depth
    part = block // parts
    cut = min(span, block)

    def remote(src, dst, s, r, dev):
        return pltpu.make_async_remote_copy(src_ref=src, dst_ref=dst, send_sem=s, recv_sem=r, device_id=dev,
                                            device_id_type=MESH)

    def device(r, c):
        return {"dp": (r * width + c) * 2 + core}

    def shift_row(d):
        return lax.rem(row + d, height)

    def shift_col(d):
        return lax.rem(col + d, width)

    load_x = pltpu.make_async_copy(x_hbm, x, load_sem)

    def load_w(h, k):
        return pltpu.make_async_copy(w_hbm.at[:, k, h], w.at[:, h, k], load_w_sem.at[h, k])

    def piece_of(peer, h, k):
        return dkv_hbm.at[peer, :, pl.ds((k * parts + h) * span, span)]

    def own_copy(h, k):
        return pltpu.make_async_copy(piece_of(me, h, k), slots.at[z, h, k, 0], own_sem.at[h, k])

    for h, k in order:
        own_copy(h, k).start()
    load_x.start()
    for h, k in order:
        load_w(h, k).start()

    barrier = pltpu.get_barrier_semaphore()
    for d in range(1, dp_count):
        pl.semaphore_signal(barrier, inc=1, device_id={"dp": lax.rem(me + d, dp_count)}, device_id_type=MESH)
    for d in range(1, depth):
        pl.semaphore_signal(barrier, inc=1, device_id={"tensor": lax.rem(z + d, depth)}, device_id_type=MESH)
    pl.semaphore_wait(barrier, dp_count - 1 + depth - 1)

    def cot_copy(d, h, k):
        peer = lax.rem(me + d, dp_count)
        return remote(piece_of(peer, h, k), slots.at[z, h, k, d], a2a_s.at[d - 1, h, k], a2a_r.at[d - 1, h, k],
                      {"dp": peer})

    for h, k in order:
        for d in range(1, dp_count):
            cot_copy(d, h, k).start()

    def right_copy(step, h, k):
        ref = slots.at[z - step, h, k]
        return remote(ref, ref, right_s.at[step, h, k], right_r.at[step, h, k], {"tensor": z + 1})

    def left_copy(step, h, k):
        ref = slots.at[z + step, h, k]
        return remote(ref, ref, left_s.at[step, h, k], left_r.at[step, h, k], {"tensor": z - 1})

    def wait_right(step, h, k):
        ref = slots.at[z - step, h, k]
        remote(ref, ref, right_s.at[step, h, k], right_r.at[step - 1, h, k], {"tensor": z - 1}).wait_recv()

    def wait_left(step, h, k):
        ref = slots.at[z + step, h, k]
        remote(ref, ref, left_s.at[step, h, k], left_r.at[step - 1, h, k], {"tensor": z + 1}).wait_recv()

    for h, k in order:
        own_copy(h, k).wait()
        for d in range(1, dp_count):
            cot_copy(d, h, k).wait_recv()

        @pl.when(z < depth - 1)
        def _(h=h, k=k):
            right_copy(0, h, k).start()

        @pl.when(z > 0)
        def _(h=h, k=k):
            left_copy(0, h, k).start()

    chunk = 64

    def over_tiles(body, wide):
        def outer(i, carry):
            at = pl.ds(pl.multiple_of(i * chunk, chunk), chunk)

            def inner(j, inner_carry):
                body(at, pl.ds(pl.multiple_of(j * wide, wide), wide))
                return inner_carry

            return lax.fori_loop(0, features // wide, inner, carry)

        lax.fori_loop(0, rows // chunk, outer, 0)

    def row_sums(body, which):
        def outer(i, carry):
            at = pl.ds(pl.multiple_of(i * chunk, chunk), chunk)

            def inner(j, acc):
                return acc + body(at, pl.ds(pl.multiple_of(j * 128, 128), 128))

            lanes[at, :] = lax.fori_loop(0, features // 128, inner, jnp.zeros((chunk, 128), F32), unroll=4)
            return carry

        lax.fori_loop(0, rows // chunk, outer, 0)
        sums = jnp.sum(lanes[...].T, axis=0, keepdims=True)
        sstat[which] = jnp.broadcast_to(sums, (8, rows))
        for d in range(1, depth):
            stat_copy(which, d).start()

    def stat_copy(which, d):
        return remote(sstat.at[which], rstat.at[which, d - 1], stat_s.at[which, d - 1], stat_r.at[which, d - 1],
                      {"tensor": lax.rem(z + d, depth)})

    def row_total(which):
        value = sstat[which]
        for d in range(1, depth):
            stat_copy(which, d).wait_recv()
            value += rstat[which, d - 1]
        return value[0:1, :]

    def as_column(value):
        return jnp.broadcast_to(value, (128, rows)).T

    load_x.wait()

    def square(at, wide):
        values = x[at, wide].astype(F32)
        return values * values

    row_sums(square, 0)

    dest = dest_ref[...]
    dest_col = as_column(dest.astype(F32))[:, 0:1]
    first = lax.broadcasted_iota(jnp.int32, (rows, rows), 0)
    second_axis = lax.broadcasted_iota(jnp.int32, (rows, rows), 1)
    same = (dest_col == dest.astype(F32)) & (first < second_axis)
    rank = jnp.sum(jnp.where(same, 1.0, 0.0), axis=0, keepdims=True)
    offset = me - dest
    offset = jnp.where(offset < 0, offset + dp_count, offset)
    position = jnp.where(dest >= 0, offset.astype(F32) * peer_rows + rank, -1.0)
    place_t[...] = jnp.where(position.astype(jnp.int32) == first, 1.0, 0.0).astype(BF)
    position_col = as_column(position)[:, 0:1].astype(jnp.int32)
    place[...] = jnp.where(position_col == second_axis, 1.0, 0.0).astype(BF)

    def pair_copy(index, h):
        at = pl.ds(h * part, part)
        return remote(cot_t.at[index, 1 - core, at], rcot.at[index, at], pair_s.at[index, h], pair_r.at[index, h],
                      {"dp": sibling})

    def rows_of(h):
        if isinstance(h, int):
            return pl.ds(h * part, part)
        return pl.ds(pl.multiple_of(h * part, part), part)

    def consume(b, h, fresh):
        block_slots = jnp.concatenate([slots[b, h, k].reshape(rows, span) for k in range(lists)], axis=1)
        cot_rows = lax.dot_general(block_slots, place_t[...], (((0,), (0,)), ((), ())),
                                   preferred_element_type=F32).astype(BF)
        for k in range(lists):
            for i in range(0, span, cut):
                start = k * parts * span + i
                cot_t[b * chips_each + start // (2 * block), (start // block) % 2,
                      pl.ds(h * span + start % block, cut)] = cot_rows[k * span + i:k * span + i + cut]
        for q in range(chips_each):
            pair_copy(b * chips_each + q, h).start()
        cot_buf[...] = jnp.dot(place[...], block_slots, preferred_element_type=F32).astype(BF)

        def step(i, carry):
            at = pl.ds(pl.multiple_of(i * tile, tile), tile)
            value = jnp.dot(cot_buf[...], w[b, h, :, :, at].reshape(lists * span, tile), preferred_element_type=F32)
            if fresh:
                dnormed[:, at] = value
            else:
                dnormed[:, at] += value
            return carry

        lax.fori_loop(0, features // tile, step, 0)

    def product(index, h, start, store):
        def step(i, carry):
            at = pl.ds(pl.multiple_of(i * tile, tile), tile)
            wide = pl.ds(pl.multiple_of(start + i * tile, tile), tile)
            value = jnp.dot(cot_t[index, core, rows_of(h)], normed[:, wide], preferred_element_type=F32)
            value += jnp.dot(rcot[index, rows_of(h)], rnormed[:, wide], preferred_element_type=F32)
            store(at, wide, value)
            return carry

        lax.fori_loop(0, half // tile, step, 0)

    def xa_copy(dc, dr, h):
        return remote(sxa.at[dc - 1, dr, h], rxa.at[dc - 1, dr, h], xa_s.at[dc - 1, dr, h], xa_r.at[dc - 1, dr, h],
                      device(row, shift_col(dc)))

    def ya_copy(dr, dc, h):
        return remote(sya.at[dr - 1, dc, h], rya.at[dr - 1, dc, h], ya_s.at[dr - 1, dc, h], ya_r.at[dr - 1, dc, h],
                      device(shift_row(dr), col))

    def xb_copy(dc, h):
        return remote(sxb.at[dc - 1, h], rxb.at[dc - 1, h], xb_s.at[dc - 1, h], xb_r.at[dc - 1, h],
                      device(row, shift_col(dc)))

    def yb_copy(dr, h):
        return remote(syb.at[dr - 1, h], ryb.at[dr - 1, h], yb_s.at[dr - 1, h], yb_r.at[dr - 1, h],
                      device(shift_row(dr), col))

    def contribute(b, h):
        for q in range(chips_each):
            index = b * chips_each + q
            dr = lax.rem(index // width - row + height, height)
            dc = lax.rem(lax.rem(index, width) - col + width, width)
            pair_copy(index, h).wait_recv()

            @pl.when(dc > 0)
            def _():
                def store(at, wide, value):
                    sxa[dc - 1, dr, h, :, at] = value.astype(BF)

                product(index, h, 0, store)
                xa_copy(dc, dr, h).start()

            @pl.when(dr > 0)
            def _():
                def store(at, wide, value):
                    sya[dr - 1, dc, h, :, at] = value.astype(BF)

                product(index, h, half, store)
                ya_copy(dr, dc, h).start()

    def second_stage(h):
        for dr in range(1, height):
            for dc in range(1, width):
                xa_copy(dc, dr, h).wait_recv()

            def store(at, wide, value, dr=dr):
                for dc in range(1, width):
                    value += rxa[dc - 1, dr, h, :, at].astype(F32)
                syb[dr - 1, h, :, at] = value.astype(BF)

            product(shift_row(dr) * width + col, h, 0, store)
            yb_copy(dr, h).start()
        for dc in range(1, width):
            for dr in range(1, height):
                ya_copy(dr, dc, h).wait_recv()

            def store(at, wide, value, dc=dc):
                for dr in range(1, height):
                    value += rya[dr - 1, dc, h, :, at].astype(F32)
                sxb[dc - 1, h, :, at] = value.astype(BF)

            product(row * width + shift_col(dc), h, half, store)
            xb_copy(dc, h).start()

    for h, k in order:
        load_w(h, k).wait()
    for h in range(parts):
        consume(z, h, h == 0)

    inverse = lax.rsqrt(row_total(0) / D + EPS)
    inv_col[...] = as_column(inverse)

    def normalize(at, wide):
        values = x[at, wide].astype(F32)
        normed[at, wide] = (values * inv_col[at, 0:1] * gain_ref[:, wide].astype(F32)).astype(BF)

    wide_tile = min(512, features)
    over_tiles(normalize, wide_tile)
    share = remote(normed, rnormed, nrm_s, nrm_r, {"dp": sibling})
    share.start()

    last = parts * (depth - 1) - 1

    def chain(unit, carry):
        h = unit // (depth - 1)
        step = 1 + lax.rem(unit, depth - 1)

        @pl.when(unit == last)
        def _():
            for done in range(parts - 1):
                second_stage(done)

        for k in range(lists):
            @pl.when(z - step >= 0)
            def _(k=k):
                wait_right(step, h, k)

                @pl.when(z < depth - 1)
                def _():
                    right_copy(step, h, k).start()

            @pl.when(z + step <= depth - 1)
            def _(k=k):
                wait_left(step, h, k)

                @pl.when(z > 0)
                def _():
                    left_copy(step, h, k).start()

        @pl.when(z - step >= 0)
        def _():
            consume(z - step, h, False)

        @pl.when(z + step <= depth - 1)
        def _():
            consume(z + step, h, False)

        @pl.when(unit == 0)
        def _():
            share.wait_recv()
            for done in range(parts):
                contribute(z, done)

        @pl.when(z - step >= 0)
        def _():
            contribute(z - step, h)

        @pl.when(z + step <= depth - 1)
        def _():
            contribute(z + step, h)

        return carry

    lax.fori_loop(0, parts * (depth - 1), chain, 0)

    def dotted(at, wide):
        return x[at, wide].astype(F32) * gain_ref[:, wide].astype(F32) * dnormed[at, wide]

    row_sums(dotted, 1)

    for h in range(parts):
        def keep(at, wide, value, h=h):
            total[rows_of(h), wide] = value

        product(chip, h, 0, keep)
        product(chip, h, half, keep)

    second_stage(parts - 1)

    inverse_row = lax.rsqrt(row_total_done(sstat, rstat, depth) / D + EPS)
    fac_col[...] = as_column(inverse_row**3 * (row_total(1) / D))

    def gradient(at, wide):
        values = x[at, wide].astype(F32)
        gx[at, wide] = (inv_col[at, 0:1] * gain_ref[:, wide].astype(F32) * dnormed[at, wide]
                        - values * fac_col[at, 0:1]).astype(BF)

    over_tiles(gradient, wide_tile)
    store_gx = pltpu.make_async_copy(gx, gx_hbm, store_sem.at[0])
    store_gx.start()

    stores = []
    for h in range(parts):
        for dc in range(1, width):
            xa_copy(dc, 0, h).wait_recv()
            xb_copy(dc, h).wait_recv()
        for dr in range(1, height):
            ya_copy(dr, 0, h).wait_recv()
            yb_copy(dr, h).wait_recv()

        def finish(i, carry, h=h):
            at = pl.ds(pl.multiple_of(i * tile, tile), tile)
            wide = pl.ds(pl.multiple_of(half + i * tile, tile), tile)
            left, right = total[rows_of(h), at], total[rows_of(h), wide]
            for dc in range(1, width):
                left += rxa[dc - 1, 0, h, :, at].astype(F32)
                right += rxb[dc - 1, h, :, at].astype(F32)
            for dr in range(1, height):
                left += ryb[dr - 1, h, :, at].astype(F32)
                right += rya[dr - 1, 0, h, :, at].astype(F32)
            total[rows_of(h), at] = left
            total[rows_of(h), wide] = right
            return carry

        lax.fori_loop(0, half // tile, finish, 0)
        store_gw = pltpu.make_async_copy(total.at[rows_of(h)], gw_hbm.at[rows_of(h)], store_sem.at[1 + h])
        store_gw.start()
        stores.append(store_gw)

    for h, k in order:
        for d in range(1, dp_count):
            cot_copy(d, h, k).wait_send()
    for which in range(2):
        for d in range(1, depth):
            stat_copy(which, d).wait_send()

    def drain(step, carry):
        for h, k in order:
            @pl.when((z - step >= 0) & (z < depth - 1))
            def _(h=h, k=k):
                right_copy(step, h, k).wait_send()

            @pl.when((z + step <= depth - 1) & (z > 0))
            def _(h=h, k=k):
                left_copy(step, h, k).wait_send()

        return carry

    lax.fori_loop(0, depth, drain, 0)
    share.wait_send()
    for h in range(parts):
        for index in range(dp_count // 2):
            pair_copy(index, h).wait_send()
        for dc in range(1, width):
            for dr in range(height):
                xa_copy(dc, dr, h).wait_send()
            xb_copy(dc, h).wait_send()
        for dr in range(1, height):
            for dc in range(width):
                ya_copy(dr, dc, h).wait_send()
            yb_copy(dr, h).wait_send()
    store_gx.wait()
    for copy in stores:
        copy.wait()


def row_total_done(sstat, rstat, depth):
    value = sstat[0]
    for d in range(1, depth):
        value += rstat[0, d - 1]
    return value[0:1, :]


def shards(layer_input, gain, w_kv, d_kv, destination):
    dp_count, depth = lax.axis_size("dp"), lax.axis_size("tensor")
    height, width = chip_grid(dp_count)
    rows, features = layer_input.shape
    columns = d_kv.shape[1]
    chips = dp_count // 2
    block = w_kv.shape[0] // dp_count
    half = features // 2
    span = min(LANES, columns)
    parts = max(1, block // span)
    lists = columns // (span * parts)
    part = block // parts
    dma, vmem = pltpu.SemaphoreType.DMA, pltpu.VMEM
    anywhere = pl.BlockSpec(memory_space=pl.ANY)
    inside = pl.BlockSpec(memory_space=pltpu.VMEM)
    return pl.pallas_call(
        functools.partial(kernel, (dp_count, depth, height, width)),
        out_shape=(jax.ShapeDtypeStruct((rows, features), BF), jax.ShapeDtypeStruct((block, features), F32)),
        in_specs=[anywhere, inside, anywhere, anywhere, inside],
        out_specs=(anywhere, anywhere),
        scratch_shapes=[
            vmem((rows, features), BF),
            vmem((depth, parts, lists, span, features), BF),
            vmem((depth, parts, lists, dp_count, rows // dp_count, span), BF),
            vmem((rows, rows), BF),
            vmem((rows, rows), BF),
            vmem((rows, lists * span), BF),
            vmem((chips, 2, block, rows), BF),
            vmem((chips, block, rows), BF),
            vmem((rows, features), BF),
            vmem((rows, features), BF),
            vmem((rows, features), F32),
            vmem((rows, features), BF),
            vmem((block, features), F32),
            vmem((rows, 128), F32),
            vmem((rows, 128), F32),
            vmem((rows, 128), F32),
            vmem((2, 8, rows), F32),
            vmem((2, depth - 1, 8, rows), F32),
            vmem((width - 1, height, parts, part, half), BF),
            vmem((width - 1, height, parts, part, half), BF),
            vmem((height - 1, width, parts, part, half), BF),
            vmem((height - 1, width, parts, part, half), BF),
            vmem((width - 1, parts, part, half), BF),
            vmem((width - 1, parts, part, half), BF),
            vmem((height - 1, parts, part, half), BF),
            vmem((height - 1, parts, part, half), BF),
            dma, dma((parts, lists)), dma((1 + parts,)), dma((parts, lists)),
            dma((dp_count - 1, parts, lists)), dma((dp_count - 1, parts, lists)),
            dma((depth, parts, lists)), dma((depth, parts, lists)),
            dma((depth, parts, lists)), dma((depth, parts, lists)),
            dma((2, depth - 1)), dma((2, depth - 1)),
            dma((chips, parts)), dma((chips, parts)), dma, dma,
            dma((width - 1, height, parts)), dma((width - 1, height, parts)),
            dma((height - 1, width, parts)), dma((height - 1, width, parts)),
            dma((width - 1, parts)), dma((width - 1, parts)),
            dma((height - 1, parts)), dma((height - 1, parts)),
        ],
        compiler_params=pltpu.CompilerParams(collective_id=0, has_side_effects=True,
                                             vmem_limit_bytes=56 * 1024 * 1024),
    )(layer_input, gain.reshape(1, features), w_kv.reshape(depth, lists, parts, span, features),
      d_kv.reshape(dp_count, rows // dp_count, columns), destination.reshape(1, rows))


def solution(mesh):
    return jax.shard_map(
        shards,
        mesh=mesh,
        in_specs=(P("dp", "tensor"), P("tensor"), P(None, "tensor"), P("dp", "tensor"), P("dp")),
        out_specs=(P("dp", "tensor"), P("dp", "tensor")),
        check_vma=False,
    )
```

```python
import functools

import jax
import jax.numpy as jnp
from jax import lax
from jax.experimental import pallas as pl
from jax.experimental.pallas import tpu as pltpu
from jax.sharding import PartitionSpec as P

D = 8192
EPS = 1e-06
BF = jnp.bfloat16
F32 = jnp.float32


def chip_grid(dp_count):
    chips = dp_count // 2
    width = 1 << ((chips.bit_length() - 1) // 2)
    return chips // width, width


MESH = pl.DeviceIdType.MESH
LANES = 128


def kernel(shape, x_hbm, gain_ref, w_hbm, dkv_hbm, dest_ref, gx_hbm, gw_hbm,
           x, w, slots, place, place_t, cot_buf, cot_t, rcot, normed, rnormed, dnormed, gx, total,
           gain_row, lanes, inv_col, fac_col, sstat, rstat,
           sxa, rxa, sya, rya, sxb, rxb, syb, ryb,
           load_sem, load_w_sem, store_sem, own_sem, a2a_s, a2a_r, right_s, right_r, left_s, left_r, stat_s, stat_r,
           pair_s, pair_r, nrm_s, nrm_r, xa_s, xa_r, ya_s, ya_r, xb_s, xb_r, yb_s, yb_r):
    dp_count, depth, height, width = shape
    me = lax.axis_index("dp")
    z = lax.axis_index("tensor")
    core = lax.rem(me, 2)
    chip = me // 2
    row, col = chip // width, lax.rem(chip, width)
    sibling = me + 1 - 2 * core
    rows, features = x.shape
    parts, lists, peer_rows, span = slots.shape[1], slots.shape[2], slots.shape[4], slots.shape[5]
    order = [(h, k) for h in range(parts) for k in range(lists)]
    block = total.shape[0]
    half = features // 2
    tile = min(256, half)
    chips_each = (dp_count // 2) // depth
    part = block // parts
    cut = min(span, block)

    def remote(src, dst, s, r, dev):
        return pltpu.make_async_remote_copy(src_ref=src, dst_ref=dst, send_sem=s, recv_sem=r, device_id=dev,
                                            device_id_type=MESH)

    def device(r, c):
        return {"dp": (r * width + c) * 2 + core}

    def shift_row(d):
        return lax.rem(row + d, height)

    def shift_col(d):
        return lax.rem(col + d, width)

    load_x = pltpu.make_async_copy(x_hbm, x, load_sem)

    def load_w(h, k):
        return pltpu.make_async_copy(w_hbm.at[:, k, h], w.at[:, h, k], load_w_sem.at[h, k])

    def piece_of(peer, h, k):
        return dkv_hbm.at[peer, :, pl.ds((k * parts + h) * span, span)]

    def own_copy(h, k):
        return pltpu.make_async_copy(piece_of(me, h, k), slots.at[z, h, k, 0], own_sem.at[h, k])

    for h, k in order:
        own_copy(h, k).start()
    load_x.start()
    for h, k in order:
        load_w(h, k).start()

    barrier = pltpu.get_barrier_semaphore()
    for d in range(1, dp_count):
        pl.semaphore_signal(barrier, inc=1, device_id={"dp": lax.rem(me + d, dp_count)}, device_id_type=MESH)
    for d in range(1, depth):
        pl.semaphore_signal(barrier, inc=1, device_id={"tensor": lax.rem(z + d, depth)}, device_id_type=MESH)
    pl.semaphore_wait(barrier, dp_count - 1 + depth - 1)

    def cot_copy(d, h, k):
        peer = lax.rem(me + d, dp_count)
        return remote(piece_of(peer, h, k), slots.at[z, h, k, d], a2a_s.at[d - 1, h, k], a2a_r.at[d - 1, h, k],
                      {"dp": peer})

    for h, k in order:
        for d in range(1, dp_count):
            cot_copy(d, h, k).start()

    def right_copy(step, h, k):
        ref = slots.at[z - step, h, k]
        return remote(ref, ref, right_s.at[step, h, k], right_r.at[step, h, k], {"tensor": z + 1})

    def left_copy(step, h, k):
        ref = slots.at[z + step, h, k]
        return remote(ref, ref, left_s.at[step, h, k], left_r.at[step, h, k], {"tensor": z - 1})

    def wait_right(step, h, k):
        ref = slots.at[z - step, h, k]
        remote(ref, ref, right_s.at[step, h, k], right_r.at[step - 1, h, k], {"tensor": z - 1}).wait_recv()

    def wait_left(step, h, k):
        ref = slots.at[z + step, h, k]
        remote(ref, ref, left_s.at[step, h, k], left_r.at[step - 1, h, k], {"tensor": z + 1}).wait_recv()

    def launch(h, k):
        own_copy(h, k).wait()
        for d in range(1, dp_count):
            cot_copy(d, h, k).wait_recv()

        @pl.when(z < depth - 1)
        def _():
            right_copy(0, h, k).start()

        @pl.when(z > 0)
        def _():
            left_copy(0, h, k).start()

    launch(*order[0])

    chunk = 64

    def over_tiles(body, wide):
        def outer(i, carry):
            at = pl.ds(pl.multiple_of(i * chunk, chunk), chunk)

            def inner(j, inner_carry):
                body(at, pl.ds(pl.multiple_of(j * wide, wide), wide))
                return inner_carry

            return lax.fori_loop(0, features // wide, inner, carry)

        lax.fori_loop(0, rows // chunk, outer, 0)

    def row_sums(body, which):
        def outer(i, carry):
            at = pl.ds(pl.multiple_of(i * chunk, chunk), chunk)

            def inner(j, acc):
                return acc + body(at, pl.ds(pl.multiple_of(j * 128, 128), 128))

            lanes[at, :] = lax.fori_loop(0, features // 128, inner, jnp.zeros((chunk, 128), F32), unroll=4)
            return carry

        lax.fori_loop(0, rows // chunk, outer, 0)
        sums = jnp.sum(lanes[...].T, axis=0, keepdims=True)
        sstat[which] = jnp.broadcast_to(sums, (8, rows))
        for d in range(1, depth):
            stat_copy(which, d).start()

    def stat_copy(which, d):
        return remote(sstat.at[which], rstat.at[which, d - 1], stat_s.at[which, d - 1], stat_r.at[which, d - 1],
                      {"tensor": lax.rem(z + d, depth)})

    def row_total(which):
        value = sstat[which]
        for d in range(1, depth):
            stat_copy(which, d).wait_recv()
            value += rstat[which, d - 1]
        return value[0:1, :]

    def as_column(value):
        return jnp.broadcast_to(value, (128, rows)).T

    gain_row[...] = gain_ref[...].astype(F32).reshape(1, features)
    load_x.wait()

    def square(at, wide):
        values = x[at, wide].astype(F32)
        return values * values

    row_sums(square, 0)
    for h, k in order[1:2]:
        launch(h, k)

    dest = dest_ref[...]
    dest_col = as_column(dest.astype(F32))[:, 0:1]
    first = lax.broadcasted_iota(jnp.int32, (rows, rows), 0)
    second_axis = lax.broadcasted_iota(jnp.int32, (rows, rows), 1)
    same = (dest_col == dest.astype(F32)) & (first < second_axis)
    rank = jnp.sum(jnp.where(same, 1.0, 0.0), axis=0, keepdims=True)
    offset = me - dest
    offset = jnp.where(offset < 0, offset + dp_count, offset)
    position = jnp.where(dest >= 0, offset.astype(F32) * peer_rows + rank, -1.0)
    place_t[...] = jnp.where(position.astype(jnp.int32) == first, 1.0, 0.0).astype(BF)
    position_col = as_column(position)[:, 0:1].astype(jnp.int32)
    place[...] = jnp.where(position_col == second_axis, 1.0, 0.0).astype(BF)

    for h, k in order[2:]:
        launch(h, k)

    def pair_copy(index, h):
        at = pl.ds(h * part, part)
        return remote(cot_t.at[index, 1 - core, at], rcot.at[index, at], pair_s.at[index, h], pair_r.at[index, h],
                      {"dp": sibling})

    def rows_of(h):
        if isinstance(h, int):
            return pl.ds(h * part, part)
        return pl.ds(pl.multiple_of(h * part, part), part)

    def consume(b, h, fresh):
        block_slots = jnp.concatenate([slots[b, h, k].reshape(rows, span) for k in range(lists)], axis=1)
        cot_rows = lax.dot_general(block_slots, place_t[...], (((0,), (0,)), ((), ())),
                                   preferred_element_type=F32).astype(BF)
        for k in range(lists):
            for i in range(0, span, cut):
                start = k * parts * span + i
                cot_t[b * chips_each + start // (2 * block), (start // block) % 2,
                      pl.ds(h * span + start % block, cut)] = cot_rows[k * span + i:k * span + i + cut]
        for q in range(chips_each):
            pair_copy(b * chips_each + q, h).start()
        cot_buf[...] = jnp.dot(place[...], block_slots, preferred_element_type=F32).astype(BF)

        def step(i, carry):
            at = pl.ds(pl.multiple_of(i * tile, tile), tile)
            value = jnp.dot(cot_buf[...], w[b, h, :, :, at].reshape(lists * span, tile), preferred_element_type=F32)
            if fresh:
                dnormed[:, at] = value
            else:
                dnormed[:, at] += value
            return carry

        lax.fori_loop(0, features // tile, step, 0)

    def product(index, h, start, store):
        def step(i, carry):
            at = pl.ds(pl.multiple_of(i * tile, tile), tile)
            wide = pl.ds(pl.multiple_of(start + i * tile, tile), tile)
            value = jnp.dot(cot_t[index, core, rows_of(h)], normed[:, wide], preferred_element_type=F32)
            value += jnp.dot(rcot[index, rows_of(h)], rnormed[:, wide], preferred_element_type=F32)
            store(at, wide, value)
            return carry

        lax.fori_loop(0, half // tile, step, 0)

    def xa_copy(dc, dr, h):
        return remote(sxa.at[dc - 1, dr, h], rxa.at[dc - 1, dr, h], xa_s.at[dc - 1, dr, h], xa_r.at[dc - 1, dr, h],
                      device(row, shift_col(dc)))

    def ya_copy(dr, dc, h):
        return remote(sya.at[dr - 1, dc, h], rya.at[dr - 1, dc, h], ya_s.at[dr - 1, dc, h], ya_r.at[dr - 1, dc, h],
                      device(shift_row(dr), col))

    def xb_copy(dc, h):
        return remote(sxb.at[dc - 1, h], rxb.at[dc - 1, h], xb_s.at[dc - 1, h], xb_r.at[dc - 1, h],
                      device(row, shift_col(dc)))

    def yb_copy(dr, h):
        return remote(syb.at[dr - 1, h], ryb.at[dr - 1, h], yb_s.at[dr - 1, h], yb_r.at[dr - 1, h],
                      device(shift_row(dr), col))

    def contribute(b, h):
        for q in range(chips_each):
            index = b * chips_each + q
            dr = lax.rem(index // width - row + height, height)
            dc = lax.rem(lax.rem(index, width) - col + width, width)
            pair_copy(index, h).wait_recv()

            @pl.when(dc > 0)
            def _():
                def store(at, wide, value):
                    sxa[dc - 1, dr, h, :, at] = value.astype(BF)

                product(index, h, 0, store)
                xa_copy(dc, dr, h).start()

            @pl.when(dr > 0)
            def _():
                def store(at, wide, value):
                    sya[dr - 1, dc, h, :, at] = value.astype(BF)

                product(index, h, half, store)
                ya_copy(dr, dc, h).start()

    def second_stage(h):
        for dr in range(1, height):
            for dc in range(1, width):
                xa_copy(dc, dr, h).wait_recv()

            def store(at, wide, value, dr=dr):
                for dc in range(1, width):
                    value += rxa[dc - 1, dr, h, :, at].astype(F32)
                syb[dr - 1, h, :, at] = value.astype(BF)

            product(shift_row(dr) * width + col, h, 0, store)
            yb_copy(dr, h).start()
        for dc in range(1, width):
            for dr in range(1, height):
                ya_copy(dr, dc, h).wait_recv()

            def store(at, wide, value, dc=dc):
                for dr in range(1, height):
                    value += rya[dr - 1, dc, h, :, at].astype(F32)
                sxb[dc - 1, h, :, at] = value.astype(BF)

            product(row * width + shift_col(dc), h, half, store)
            xb_copy(dc, h).start()

    inverse = lax.rsqrt(row_total(0) / D + EPS)
    inv_col[...] = as_column(inverse)

    def normalize(at, wide):
        values = x[at, wide].astype(F32)
        normed[at, wide] = (values * inv_col[at, 0:1] * gain_row[:, wide]).astype(BF)

    wide_tile = min(512, features)
    over_tiles(normalize, wide_tile)
    share = remote(normed, rnormed, nrm_s, nrm_r, {"dp": sibling})
    share.start()
    for h, k in order:
        load_w(h, k).wait()
    consume(z, 0, True)

    last = parts * (depth - 1) - 1

    def chain(unit, carry):
        h = unit // (depth - 1)
        step = 1 + lax.rem(unit, depth - 1)

        @pl.when(unit == last)
        def _():
            for done in range(parts - 1):
                second_stage(done)

        for k in range(lists):
            @pl.when(z - step >= 0)
            def _(k=k):
                wait_right(step, h, k)

                @pl.when(z < depth - 1)
                def _():
                    right_copy(step, h, k).start()

            @pl.when(z + step <= depth - 1)
            def _(k=k):
                wait_left(step, h, k)

                @pl.when(z > 0)
                def _():
                    left_copy(step, h, k).start()

        @pl.when(unit == 0)
        def _():
            share.wait_recv()
            contribute(z, 0)
            for more in range(1, parts):
                consume(z, more, False)

        @pl.when(z - step >= 0)
        def _():
            consume(z - step, h, False)

        @pl.when(z + step <= depth - 1)
        def _():
            consume(z + step, h, False)

        @pl.when(unit == 0)
        def _():
            for more in range(1, parts):
                contribute(z, more)

        @pl.when(z - step >= 0)
        def _():
            contribute(z - step, h)

        @pl.when(z + step <= depth - 1)
        def _():
            contribute(z + step, h)

        return carry

    lax.fori_loop(0, parts * (depth - 1), chain, 0)

    def dotted(at, wide):
        return x[at, wide].astype(F32) * gain_row[:, wide] * dnormed[at, wide]

    row_sums(dotted, 1)

    for h in range(parts):
        def keep(at, wide, value, h=h):
            total[rows_of(h), wide] = value

        product(chip, h, 0, keep)
        product(chip, h, half, keep)

    second_stage(parts - 1)

    inverse_row = lax.rsqrt(row_total_done(sstat, rstat, depth) / D + EPS)
    fac_col[...] = as_column(inverse_row**3 * (row_total(1) / D))

    def gradient(at, wide):
        values = x[at, wide].astype(F32)
        gx[at, wide] = (inv_col[at, 0:1] * gain_row[:, wide] * dnormed[at, wide]
                        - values * fac_col[at, 0:1]).astype(BF)

    over_tiles(gradient, wide_tile)
    store_gx = pltpu.make_async_copy(gx, gx_hbm, store_sem.at[0])
    store_gx.start()

    stores = []
    for h in range(parts):
        for dc in range(1, width):
            xa_copy(dc, 0, h).wait_recv()
            xb_copy(dc, h).wait_recv()
        for dr in range(1, height):
            ya_copy(dr, 0, h).wait_recv()
            yb_copy(dr, h).wait_recv()

        def finish(i, carry, h=h):
            at = pl.ds(pl.multiple_of(i * tile, tile), tile)
            wide = pl.ds(pl.multiple_of(half + i * tile, tile), tile)
            left, right = total[rows_of(h), at], total[rows_of(h), wide]
            for dc in range(1, width):
                left += rxa[dc - 1, 0, h, :, at].astype(F32)
                right += rxb[dc - 1, h, :, at].astype(F32)
            for dr in range(1, height):
                left += ryb[dr - 1, h, :, at].astype(F32)
                right += rya[dr - 1, 0, h, :, at].astype(F32)
            total[rows_of(h), at] = left
            total[rows_of(h), wide] = right
            return carry

        lax.fori_loop(0, half // tile, finish, 0)
        store_gw = pltpu.make_async_copy(total.at[rows_of(h)], gw_hbm.at[rows_of(h)], store_sem.at[1 + h])
        store_gw.start()
        stores.append(store_gw)

    for h, k in order:
        for d in range(1, dp_count):
            cot_copy(d, h, k).wait_send()
    for which in range(2):
        for d in range(1, depth):
            stat_copy(which, d).wait_send()

    def drain(step, carry):
        for h, k in order:
            @pl.when((z - step >= 0) & (z < depth - 1))
            def _(h=h, k=k):
                right_copy(step, h, k).wait_send()

            @pl.when((z + step <= depth - 1) & (z > 0))
            def _(h=h, k=k):
                left_copy(step, h, k).wait_send()

        return carry

    lax.fori_loop(0, depth, drain, 0)
    share.wait_send()
    for h in range(parts):
        for index in range(dp_count // 2):
            pair_copy(index, h).wait_send()
        for dc in range(1, width):
            for dr in range(height):
                xa_copy(dc, dr, h).wait_send()
            xb_copy(dc, h).wait_send()
        for dr in range(1, height):
            for dc in range(width):
                ya_copy(dr, dc, h).wait_send()
            yb_copy(dr, h).wait_send()
    store_gx.wait()
    for copy in stores:
        copy.wait()


def row_total_done(sstat, rstat, depth):
    value = sstat[0]
    for d in range(1, depth):
        value += rstat[0, d - 1]
    return value[0:1, :]


def shards(layer_input, gain, w_kv, d_kv, destination):
    dp_count, depth = lax.axis_size("dp"), lax.axis_size("tensor")
    height, width = chip_grid(dp_count)
    rows, features = layer_input.shape
    columns = d_kv.shape[1]
    chips = dp_count // 2
    block = w_kv.shape[0] // dp_count
    half = features // 2
    span = min(LANES, columns)
    parts = max(1, block // span)
    lists = columns // (span * parts)
    part = block // parts
    dma, vmem = pltpu.SemaphoreType.DMA, pltpu.VMEM
    anywhere = pl.BlockSpec(memory_space=pl.ANY)
    inside = pl.BlockSpec(memory_space=pltpu.VMEM)
    return pl.pallas_call(
        functools.partial(kernel, (dp_count, depth, height, width)),
        out_shape=(jax.ShapeDtypeStruct((rows, features), BF), jax.ShapeDtypeStruct((block, features), F32)),
        in_specs=[anywhere, inside, anywhere, anywhere, inside],
        out_specs=(anywhere, anywhere),
        scratch_shapes=[
            vmem((rows, features), BF),
            vmem((depth, parts, lists, span, features), BF),
            vmem((depth, parts, lists, dp_count, rows // dp_count, span), BF),
            vmem((rows, rows), BF),
            vmem((rows, rows), BF),
            vmem((rows, lists * span), BF),
            vmem((chips, 2, block, rows), BF),
            vmem((chips, block, rows), BF),
            vmem((rows, features), BF),
            vmem((rows, features), BF),
            vmem((rows, features), F32),
            vmem((rows, features), BF),
            vmem((block, features), F32),
            vmem((1, features), F32),
            vmem((rows, 128), F32),
            vmem((rows, 128), F32),
            vmem((rows, 128), F32),
            vmem((2, 8, rows), F32),
            vmem((2, depth - 1, 8, rows), F32),
            vmem((width - 1, height, parts, part, half), BF),
            vmem((width - 1, height, parts, part, half), BF),
            vmem((height - 1, width, parts, part, half), BF),
            vmem((height - 1, width, parts, part, half), BF),
            vmem((width - 1, parts, part, half), BF),
            vmem((width - 1, parts, part, half), BF),
            vmem((height - 1, parts, part, half), BF),
            vmem((height - 1, parts, part, half), BF),
            dma, dma((parts, lists)), dma((1 + parts,)), dma((parts, lists)),
            dma((dp_count - 1, parts, lists)), dma((dp_count - 1, parts, lists)),
            dma((depth, parts, lists)), dma((depth, parts, lists)),
            dma((depth, parts, lists)), dma((depth, parts, lists)),
            dma((2, depth - 1)), dma((2, depth - 1)),
            dma((chips, parts)), dma((chips, parts)), dma, dma,
            dma((width - 1, height, parts)), dma((width - 1, height, parts)),
            dma((height - 1, width, parts)), dma((height - 1, width, parts)),
            dma((width - 1, parts)), dma((width - 1, parts)),
            dma((height - 1, parts)), dma((height - 1, parts)),
        ],
        compiler_params=pltpu.CompilerParams(collective_id=0, has_side_effects=True,
                                             vmem_limit_bytes=56 * 1024 * 1024),
    )(layer_input, gain, w_kv.reshape(depth, lists, parts, span, features),
      d_kv.reshape(dp_count, rows // dp_count, columns), destination.reshape(1, rows))


def solution(mesh):
    return jax.shard_map(
        shards,
        mesh=mesh,
        in_specs=(P("dp", "tensor"), P("tensor"), P(None, "tensor"), P("dp", "tensor"), P("dp")),
        out_specs=(P("dp", "tensor"), P("dp", "tensor")),
        check_vma=False,
    )
```
